1024 devices in a mesh: wide: 64 (over z, core), narrow: 16 (over y, x).
Axes of the slice: x: 4, y: 4, z: 32, core: 2. Of those that a mesh axis runs over, the one named last changes fastest.
Arguments:
- features: bfloat16 [16, 8192, 128], P('narrow', 'wide'), may hold values from -16 to 16
- weight: bfloat16 [128, 128], replicated, may hold values from -0.5 to 0.5
- tiles: bfloat16 [16, 8192, 8, 128], P('narrow', 'wide'), may hold values from -0.25 to 0.25
- tile_cols: int32 [16, 64, 8], P('narrow'), may hold values from 0 to 63, as said below
- tile_counts: int32 [16, 64], P('narrow'), may hold values from 2 to 8, as said below
- cotangent: bfloat16 [16, 8192, 128], P('narrow', 'wide'), may hold values from -6 to 6
Outputs:
- activated: bfloat16 [16, 8192, 128], P('narrow', 'wide')
- feature_grad: bfloat16 [16, 8192, 128], P('narrow', 'wide')
- weight_grad: float32 [128, 128], P('wide')
The draws below stay inside these ranges and needn't reach their ends.
Inputs may be any that keep to these rules, and one draw needn't show every extreme that they name: `tile_cols`: slot 0 of each block row holds that block row's own diagonal tile (its column equals the block row); other slots may name any block column of the group, also repeatedly. `tile_counts`: each group has a block row that uses all 8 slots.
All inputs are finite; a program needn't handle non-finite values.
Results may differ from the reference program's by a relative error of at most 0.0062.
Values may be sent and summed in bfloat16 or wider, within the bound.
No kernel may reach another device: no remote copies, remote signals or barrier semaphores. Data moves between devices by JAX's collectives and lax.ppermute only.
A program may use at most 32 MiB of HBM per device.

```python
import jax
import jax.numpy as jnp
from jax import lax

D = 128
TILE = 128
SLOTS = 8
GROUPS = 16
GROUP_NODES = 8192
BLOCKS = 64


def draw_tile_cols(key, part):
    key = jax.random.fold_in(key, 11)
    chosen_cols = jax.random.randint(key, (GROUPS, BLOCKS, SLOTS), 0, BLOCKS)
    own_block = jnp.broadcast_to(jnp.arange(BLOCKS, dtype=jnp.int32)[None, :, None], (GROUPS, BLOCKS, SLOTS))
    first_slot = jnp.arange(SLOTS)[None, None, :] == 0
    return jnp.where(first_slot, own_block, chosen_cols).astype(jnp.int32)


def draw_tile_counts(key, part):
    key = jax.random.fold_in(key, 12)
    key_count, key_full = jax.random.split(key)
    drawn_counts = jax.random.randint(key_count, (GROUPS, BLOCKS), 2, SLOTS + 1)
    fullest = jax.random.randint(key_full, (GROUPS,), 0, BLOCKS)
    full_row = jnp.arange(BLOCKS)[None, :] == fullest[:, None]
    return jnp.where(full_row, SLOTS, drawn_counts).astype(jnp.int32)


def raised(array, own_key, source, target, parts, factor):
    def block_of(dim):
        return (jnp.arange(array.shape[dim]) // (array.shape[dim] // parts)).reshape((-1,) + (1,) * (array.ndim - 1 - dim))

    near = jax.random.permutation(own_key, parts)[block_of(target)]
    second = (block_of(target) + parts // 2) % parts
    return jnp.where((block_of(source) == near) | (block_of(source) == second), factor * array, array)


def block_levels(own_key, extent, cuts, smallest, largest):
    gain, own = 1.0, jax.random.fold_in(own_key, 6)
    for position, blocks in cuts:
        heights = jnp.exp(jax.random.uniform(jax.random.fold_in(own, position), (blocks,), jnp.float32, smallest / len(cuts), largest / len(cuts)))
        gain = gain * jnp.repeat(heights, extent[position] // blocks).reshape([-1 if axis == position else 1 for axis in range(len(extent))])
    return gain


def noise(key, dims, scale, most, pieces=(), kind=jnp.bfloat16):
    result = scale * jax.random.normal(key, dims, jnp.float32)
    if pieces:
        result = result * block_levels(key, dims, pieces, -0.22, 0.18)
    return jnp.clip(result, -most, most).astype(kind)


def heavy_noise(key, extent, deviation, most, cuts, heavy, kind=jnp.bfloat16):
    values = deviation * jax.random.normal(key, extent, jnp.float32)
    if cuts:
        values = values * block_levels(key, extent, cuts, -0.22, 0.18)
    return jnp.clip(raised(values, jax.random.fold_in(key, 3), *heavy), -most, most).astype(kind)


def setup_inputs(seed: int = 0) -> dict:
    splits = jax.random.split(jax.random.key(seed), 7)
    features = heavy_noise(splits[0], (GROUPS, GROUP_NODES, D), 1.0, 16.0, ((0, 16), (1, 64)), (1, 2, 64, 4.0))
    weight = noise(splits[1], (D, D), D ** -0.5, 0.5)
    tiles = noise(splits[2], (GROUPS, GROUP_NODES, SLOTS, TILE), (TILE * SLOTS // 2) ** -0.5, 0.25, ((0, 16), (1, 64)))
    tile_cols = draw_tile_cols(jax.random.fold_in(splits[6], 71), 0)
    tile_counts = draw_tile_counts(jax.random.fold_in(splits[6], 71), 0)
    cotangent = noise(splits[5], (GROUPS, GROUP_NODES, D), 1.0, 6.0, ((0, 16), (1, 64)))
    return {"features": features, "weight": weight, "tiles": tiles, "tile_cols": tile_cols, "tile_counts": tile_counts, "cotangent": cotangent}


def group_pass(feat_block, weight, tile_block, col_block, count_block, cot_block):
    block_count = col_block.shape[0]
    slot_count = col_block.shape[1]
    tile_size = tile_block.shape[2]
    node_count = feat_block.shape[0]
    feat_width = feat_block.shape[1]
    projected = jnp.dot(feat_block, weight, preferred_element_type=jnp.float32).astype(jnp.bfloat16)
    alive_mask = jnp.arange(slot_count)[None, :] < count_block[:, None]
    stacked = projected.reshape(block_count, tile_size, feat_width)
    picked = stacked[col_block] * alive_mask[:, :, None, None].astype(jnp.bfloat16)
    tile_rows = tile_block.reshape(block_count, tile_size, slot_count, tile_size).astype(jnp.float32)
    pre_act = jnp.einsum('bnst,bstd->bnd', tile_rows, picked.astype(jnp.float32))
    pre_act = pre_act.reshape(node_count, feat_width)
    sig_val = jax.nn.sigmoid(pre_act)
    activated = (pre_act * sig_val).astype(jnp.bfloat16)
    act_grad = (cot_block.astype(jnp.float32) * sig_val * (1.0 + pre_act * (1.0 - sig_val))).astype(jnp.bfloat16)
    contrib = jnp.einsum('bnst,bnd->bstd', tile_rows,
                         act_grad.reshape(block_count, tile_size, feat_width).astype(jnp.float32))
    seg_ids = jnp.where(alive_mask, col_block, block_count).reshape(-1).astype(jnp.int32)
    summed = jax.ops.segment_sum(contrib.reshape(block_count * slot_count, tile_size, feat_width),
                                 seg_ids, num_segments=block_count + 1)
    proj_grad = summed[:block_count].reshape(node_count, feat_width).astype(jnp.bfloat16)
    feature_grad = jnp.dot(proj_grad, weight.T, preferred_element_type=jnp.float32).astype(jnp.bfloat16)
    weight_part = jnp.dot(feat_block.T, proj_grad, preferred_element_type=jnp.float32)
    return activated, feature_grad, weight_part


def reference(features, weight, tiles, tile_cols, tile_counts, cotangent):
    def one_group(items):
        return group_pass(items[0], weight, items[1], items[2], items[3], items[4])

    activated, feature_grad, weight_parts = lax.map(one_group, (features, tiles, tile_cols, tile_counts, cotangent))
    return activated, feature_grad, jnp.sum(weight_parts, axis=0)
```

```python
import jax
import jax.numpy as jnp
from jax import lax
from jax.experimental import pallas as pl
from jax.experimental.pallas import tpu as pltpu
from jax.sharding import PartitionSpec as P

F32 = jnp.float32
BF16 = jnp.bfloat16
VMEM = pl.BlockSpec(memory_space=pltpu.VMEM)
SMEM = pl.BlockSpec(memory_space=pltpu.SMEM)
PARAMS = pltpu.CompilerParams(vmem_limit_bytes=32 * 1024 * 1024)

NEAR = (0, 1, 2, -1)
FAR = (0, 8, 16, -8)


def forward(pos, gathered, tile_rows, weight, partial, high, low):
    slots = pos.shape[1]
    for r in range(2):
        picked = jnp.concatenate([gathered[pos[r, s]] for s in range(slots)], axis=0)
        mixed = jnp.dot(tile_rows[r], picked, preferred_element_type=F32)
        top = mixed.astype(BF16)
        rest = (mixed - top.astype(F32)).astype(BF16)
        high[r] = top
        low[r] = rest
        partial[r] = jnp.dot(top, weight[...], preferred_element_type=F32) + jnp.dot(
            rest, weight[...], preferred_element_type=F32
        )


def backward(
    pos, mine, theirs, cot, tile_cols, weight, high, low, perm,
    activated, out0, out1, out2, out3, total,
):
    slots = pos.shape[1]
    tile = weight.shape[0]
    blocks = total.shape[0] - 1
    total[...] = jnp.zeros_like(total)
    grad = jnp.zeros((tile, tile), F32)
    for r in range(2):
        pre = mine[r] + theirs[1 - r]
        sig = jax.nn.sigmoid(pre)
        if r == 0:
            activated[...] = (pre * sig).astype(BF16)
        act_grad = (cot[r].astype(F32) * sig * (1.0 + pre * (1.0 - sig))).astype(BF16)
        moved = lax.dot_general(
            act_grad, weight[...], (((1,), (1,)), ((), ())), preferred_element_type=F32
        ).astype(BF16)
        for part in (high, low):
            grad += lax.dot_general(
                part[r], act_grad, (((0,), (0,)), ((), ())), preferred_element_type=F32
            )
        for s in range(slots):
            term = jnp.dot(
                tile_cols[r, pl.ds(s * tile, tile), :], moved, preferred_element_type=F32
            )
            total[pos[r, s]] += term
    top = grad.astype(BF16)
    rest = (grad - top.astype(F32)).astype(BF16)
    ordered_top = jnp.dot(perm[...], top, preferred_element_type=F32).astype(BF16)
    ordered_rest = jnp.dot(perm[...], rest, preferred_element_type=F32).astype(BF16)
    share = blocks // 4
    rows = tile // 4
    for a, out in enumerate((out0, out1, out2, out3)):
        for k in range(share):
            out[pl.ds(k * tile, tile), :] = total[a * share + k].astype(BF16)
        out[pl.ds(share * tile, rows), :] = ordered_top[a * rows : (a + 1) * rows]
        out[pl.ds(share * tile + rows, rows), :] = ordered_rest[a * rows : (a + 1) * rows]


def split(x):
    top = x.astype(BF16)
    return jnp.concatenate([top, (x - top.astype(F32)).astype(BF16)], 0)


def shards(features, weight, tiles, tile_cols, tile_counts, cotangent):
    feat = features[0]
    tile = feat.shape[0]
    slots = tiles.shape[2]
    wide = lax.axis_size("wide")
    chips = wide // 2
    w = lax.axis_index("wide")
    z, c = w // 2, w % 2
    sign = 1 - 2 * c

    def send(x, d):
        return lax.ppermute(
            x, "wide",
            [(2 * i + k, 2 * ((i + (d if k == 0 else -d)) % chips) + k) for i in range(chips) for k in range(2)],
        )

    def swap(x):
        return lax.ppermute(x, "wide", [(i, i ^ 1) for i in range(wide)])

    with jax.named_scope("gather_far"):
        held = jnp.stack([feat] + [send(feat, d) for d in FAR[1:]])
    with jax.named_scope("prepare"):
        rows = tiles[0].reshape(tile, slots * tile)
        both = jnp.concatenate([rows, cotangent[0]], axis=1)
        other = swap(both)
        tile_rows = jnp.stack([rows, other[:, : slots * tile]])
        tile_flip = jnp.swapaxes(tile_rows, 1, 2)
        cot = jnp.stack([cotangent[0], other[:, slots * tile :]])
        here = jnp.stack([w, w ^ 1])
        cols = tile_cols[0][here]
        counts = tile_counts[0][here]
        offset = (sign * (z - cols // 2)) % chips
        near = offset % 4
        far = ((offset + 1) // 4) % (chips // 4)
        place = near * (chips // 4) + (far % 2) * 4 + far // 2
        active = (jnp.arange(slots)[None, :] < counts[:, None]) & (cols % 2 == c)
        pos = jnp.where(active, place, chips).astype(jnp.int32)
        spot = jnp.arange(chips)
        near_at = jnp.where(spot // 8 == 3, -1, spot // 8)
        chip_at = (z - sign * (near_at + 4 * (spot % 8 // 4) + 8 * (spot % 4))) % chips
        row_share = tile // chips
        row_at = (chip_at[:, None] * row_share + jnp.arange(row_share)[None, :]).reshape(-1)
        perm = (row_at[:, None] == jnp.arange(tile)[None, :]).astype(BF16)
    with jax.named_scope("gather_middle"):
        held = jnp.concatenate([held, send(held, 4)], 0)
    with jax.named_scope("gather_near"):
        gathered = jnp.concatenate(
            [held] + [send(held, d) for d in NEAR[1:]] + [jnp.zeros((1, tile, tile), BF16)], 0
        )
    square = (2, tile, tile)
    partial, high, low = pl.pallas_call(
        forward,
        out_shape=[
            jax.ShapeDtypeStruct(square, F32),
            jax.ShapeDtypeStruct(square, BF16),
            jax.ShapeDtypeStruct(square, BF16),
        ],
        in_specs=[SMEM, VMEM, VMEM, VMEM],
        out_specs=[VMEM] * 3,
        compiler_params=PARAMS,
        name="forward",
    )(pos, gathered, tile_rows, weight)
    with jax.named_scope("pair"):
        theirs = swap(partial)
    share = chips // 4
    length = share * tile + tile // 2
    activated, part0, part1, part2, part3 = pl.pallas_call(
        backward,
        out_shape=[jax.ShapeDtypeStruct((tile, tile), BF16)]
        + [jax.ShapeDtypeStruct((length, tile), BF16)] * 4,
        in_specs=[SMEM] + [VMEM] * 8,
        out_specs=[VMEM] * 5,
        scratch_shapes=[pltpu.VMEM((chips + 1, tile, tile), F32)],
        compiler_params=PARAMS,
        name="backward",
    )(pos, partial, theirs, cot, tile_flip, weight, high, low, perm)

    def add(parts, count):
        wide_parts = [p.astype(F32) for p in parts]
        whole = sum(wide_parts[1:], wide_parts[0])
        main = whole[: count * tile].astype(BF16).reshape(count, tile, tile)
        grad = whole[count * tile :]
        half = grad.shape[0] // 2
        return main, grad[:half] + grad[half:]

    with jax.named_scope("scatter_near"):
        sent = [send(p, -d) for p, d in zip((part1, part2, part3), NEAR[1:])]
        main, grad = add([part0] + sent, share)
    with jax.named_scope("scatter_middle"):
        half = main.shape[0] // 2
        cut = grad.shape[0] // 2
        message = jnp.concatenate([main[half:].reshape(half * tile, tile), split(grad[cut:])], 0)
        keep = jnp.concatenate([main[:half].reshape(half * tile, tile), split(grad[:cut])], 0)
        main, grad = add([keep, send(message, -4)], half)
    with jax.named_scope("scatter_far"):
        parts = []
        for e, d in enumerate(FAR):
            message = jnp.concatenate([main[e], split(grad[e * row_share : (e + 1) * row_share])], 0)
            parts.append(send(message, -d) if d else message)
        wide_parts = [p.astype(F32) for p in parts]
        whole = sum(wide_parts[1:], wide_parts[0])
        feature_grad = whole[:tile].astype(BF16)
        grad = whole[tile : tile + row_share] + whole[tile + row_share :]
    with jax.named_scope("weight_sum"):
        mine_rows = row_share // 2
        grad = grad.reshape(2, mine_rows, tile)
        keep = lax.dynamic_index_in_dim(grad, c, 0, keepdims=False)
        give = lax.dynamic_index_in_dim(grad, 1 - c, 0, keepdims=False)
        grad = keep + swap(give)
        groups = lax.axis_size("narrow")
        copies = lax.all_to_all(
            jnp.broadcast_to(grad[None], (groups, mine_rows, tile)), "narrow", 0, 0
        )
        weight_grad = copies.sum(0)
    return (activated[None], feature_grad[None], weight_grad)


def solution(mesh):
    placed = (
        P("narrow", "wide", None),
        P(),
        P("narrow", "wide", None, None),
        P("narrow", None, None),
        P("narrow", None),
        P("narrow", "wide", None),
    )
    return jax.shard_map(
        shards,
        mesh=mesh,
        in_specs=placed,
        out_specs=(P("narrow", "wide", None), P("narrow", "wide", None), P("wide", None)),
        check_vma=False,
    )
```

```python
import jax
import jax.numpy as jnp
from jax import lax
from jax.experimental import pallas as pl
from jax.experimental.pallas import tpu as pltpu
from jax.sharding import PartitionSpec as P

F32 = jnp.float32
BF16 = jnp.bfloat16
VMEM = pl.BlockSpec(memory_space=pltpu.VMEM)
SMEM = pl.BlockSpec(memory_space=pltpu.SMEM)
PARAMS = pltpu.CompilerParams(vmem_limit_bytes=32 * 1024 * 1024)

NEAR = (0, 1, 2, -1)
CLASSES = len(NEAR)


def forward(pos, held0, held1, held2, held3, tile_rows, mixed):
    slots = pos.shape[1]
    share = held0.shape[0]
    for r in range(2):
        picked = []
        for s in range(slots):
            near, far = pos[r, s] // share, pos[r, s] % share
            block = jnp.zeros(held0.shape[1:], BF16)
            for a, held in enumerate((held0, held1, held2, held3)):
                block = jnp.where(near == a, held[far], block)
            picked.append(block)
        mixed[r] = jnp.dot(tile_rows[r], jnp.concatenate(picked, 0), preferred_element_type=F32)


def backward(
    pos, mine, theirs, cot, tile_cols, weight, perm,
    activated, out0, out1, out2, out3, total,
):
    slots = pos.shape[1]
    tile = weight.shape[0]
    blocks = total.shape[0] - 1
    total[...] = jnp.zeros_like(total)
    grad = jnp.zeros((tile, tile), F32)
    for r in range(2):
        mixed = mine[r] + theirs[1 - r]
        high = mixed.astype(BF16)
        low = (mixed - high.astype(F32)).astype(BF16)
        pre = jnp.dot(high, weight[...], preferred_element_type=F32) + jnp.dot(
            low, weight[...], preferred_element_type=F32
        )
        sig = jax.nn.sigmoid(pre)
        if r == 0:
            activated[...] = (pre * sig).astype(BF16)
        act_grad = (cot[r].astype(F32) * sig * (1.0 + pre * (1.0 - sig))).astype(BF16)
        moved = lax.dot_general(
            act_grad, weight[...], (((1,), (1,)), ((), ())), preferred_element_type=F32
        ).astype(BF16)
        for part in (high, low):
            grad += lax.dot_general(
                part, act_grad, (((0,), (0,)), ((), ())), preferred_element_type=F32
            )
        for s in range(slots):
            term = jnp.dot(
                tile_cols[r, pl.ds(s * tile, tile), :], moved, preferred_element_type=F32
            )
            total[pos[r, s]] += term
    top = grad.astype(BF16)
    rest = (grad - top.astype(F32)).astype(BF16)
    ordered_top = jnp.dot(perm[...], top, preferred_element_type=F32).astype(BF16)
    ordered_rest = jnp.dot(perm[...], rest, preferred_element_type=F32).astype(BF16)
    share = blocks // CLASSES
    rows = perm.shape[0] // CLASSES
    for a, out in enumerate((out0, out1, out2, out3)):
        for k in range(share):
            out[pl.ds(k * tile, tile), :] = total[a * share + k].astype(BF16)
        out[pl.ds(share * tile, rows), :] = ordered_top[a * rows : (a + 1) * rows]
        out[pl.ds(share * tile + rows, rows), :] = ordered_rest[a * rows : (a + 1) * rows]


def shards(features, weight, tiles, tile_cols, tile_counts, cotangent):
    feat = features[0]
    tile = feat.shape[0]
    slots = tiles.shape[2]
    wide = lax.axis_size("wide")
    chips = wide // 2
    share = chips // CLASSES
    w = lax.axis_index("wide")
    z, c = w // 2, w % 2
    sign = 1 - 2 * c

    def send(x, d):
        return lax.ppermute(
            x, "wide",
            [(2 * i + k, 2 * ((i + (d if k == 0 else -d)) % chips) + k) for i in range(chips) for k in range(2)],
        )

    def swap(x):
        return lax.ppermute(x, "wide", [(i, i ^ 1) for i in range(wide)])

    def within_class(x):
        return lax.all_to_all(
            x, "wide", 0, 0,
            axis_index_groups=[
                [2 * (CLASSES * m + k) + core for m in range(share)] for k in range(CLASSES) for core in range(2)
            ],
        )

    with jax.named_scope("gather_far"):
        held = within_class(jnp.broadcast_to(feat[None], (share, tile, tile)))
    with jax.named_scope("prepare"):
        rows = tiles[0].reshape(tile, slots * tile)
        both = jnp.concatenate([rows, cotangent[0]], axis=1)
        other = swap(both)
        tile_rows = jnp.stack([rows, other[:, : slots * tile]])
        tile_flip = jnp.swapaxes(tile_rows, 1, 2)
        cot = jnp.stack([cotangent[0], other[:, slots * tile :]])
        here = jnp.stack([w, w ^ 1])
        cols = tile_cols[0][here]
        counts = tile_counts[0][here]
        chip = cols // 2
        place = (sign * (z - chip)) % CLASSES * share + chip // CLASSES
        active = (jnp.arange(slots)[None, :] < counts[:, None]) & (cols % 2 == c)
        pos = jnp.where(active, place, chips).astype(jnp.int32)
        spot = jnp.arange(chips)
        chip_at = (z - sign * (spot // share)) % CLASSES + CLASSES * (spot % share)
        row_share = tile // wide
        row_at = ((2 * chip_at + c)[:, None] * row_share + jnp.arange(row_share)[None, :]).reshape(-1)
        perm = (row_at[:, None] == jnp.arange(tile)[None, :]).astype(BF16)
    with jax.named_scope("gather_near"):
        gathered = [held] + [send(held, d) for d in NEAR[1:]]
    mixed = pl.pallas_call(
        forward,
        out_shape=jax.ShapeDtypeStruct((2, tile, tile), F32),
        in_specs=[SMEM] + [VMEM] * 5,
        out_specs=VMEM,
        compiler_params=PARAMS,
        name="forward",
    )(pos, *gathered, tile_rows)
    with jax.named_scope("pair"):
        theirs = swap(mixed)
    extra = share * row_share
    activated, *parts = pl.pallas_call(
        backward,
        out_shape=[jax.ShapeDtypeStruct((tile, tile), BF16)]
        + [jax.ShapeDtypeStruct((share * tile + 2 * extra, tile), BF16)] * CLASSES,
        in_specs=[SMEM] + [VMEM] * 6,
        out_specs=[VMEM] * (1 + CLASSES),
        scratch_shapes=[pltpu.VMEM((chips + 1, tile, tile), F32)],
        compiler_params=PARAMS,
        name="backward",
    )(pos, mixed, theirs, cot, tile_flip, weight, perm)
    with jax.named_scope("scatter_near"):
        whole = parts[0].astype(F32)
        for part, d in zip(parts[1:], NEAR[1:]):
            whole += send(part, -d).astype(F32)
        main = whole[: share * tile].reshape(share, tile, tile).astype(BF16)
        grad = whole[share * tile : share * tile + extra] + whole[share * tile + extra :]
        grad = grad.reshape(share, row_share, tile)
    with jax.named_scope("scatter_far"):
        top = grad.astype(BF16)
        rest = (grad - top.astype(F32)).astype(BF16)
        whole = within_class(jnp.concatenate([main, top, rest], 1)).astype(F32).sum(0)
        feature_grad = whole[:tile].astype(BF16)
        grad = whole[tile : tile + row_share] + whole[tile + row_share :]
    with jax.named_scope("weight_sum"):
        groups = lax.axis_size("narrow")
        copies = lax.all_to_all(
            jnp.broadcast_to(grad[None], (groups, row_share, tile)), "narrow", 0, 0
        )
        weight_grad = copies.sum(0)
    return (activated[None], feature_grad[None], weight_grad)


def solution(mesh):
    placed = (
        P("narrow", "wide", None),
        P(),
        P("narrow", "wide", None, None),
        P("narrow", None, None),
        P("narrow", None),
        P("narrow", "wide", None),
    )
    return jax.shard_map(
        shards,
        mesh=mesh,
        in_specs=placed,
        out_specs=(P("narrow", "wide", None), P("narrow", "wide", None), P("wide", None)),
        check_vma=False,
    )
```

```python
import jax
import jax.numpy as jnp
from jax import lax
from jax.experimental import pallas as pl
from jax.experimental.pallas import tpu as pltpu
from jax.sharding import PartitionSpec as P

F32 = jnp.float32
BF16 = jnp.bfloat16
VMEM = pl.BlockSpec(memory_space=pltpu.VMEM)
SMEM = pl.BlockSpec(memory_space=pltpu.SMEM)
PARAMS = pltpu.CompilerParams(vmem_limit_bytes=32 * 1024 * 1024)

NEAR = (0, 1, 2, -1)
CLASSES = 8


def forward(pos, own, beside, tile_rows, mixed):
    slots = pos.shape[1]
    share = own.shape[0]
    for r in range(2):
        picked = []
        for s in range(slots):
            which, far = pos[r, s] // share, pos[r, s] % share
            block = jnp.zeros(own.shape[1:], BF16)
            block = jnp.where(which == 0, own[far], block)
            block = jnp.where(which == 1, beside[far], block)
            picked.append(block)
        mixed[r] = jnp.dot(tile_rows[r], jnp.concatenate(picked, 0), preferred_element_type=F32)


def backward(
    pos, mine, theirs, cot, tile_cols, weight, perm,
    activated, out0, out1, out2, out3, total,
):
    slots = pos.shape[1]
    tile = weight.shape[0]
    blocks = total.shape[0] - 1
    total[...] = jnp.zeros_like(total)
    grad = jnp.zeros((tile, tile), F32)
    for r in range(2):
        mixed = mine[r] + theirs[1 - r]
        high = mixed.astype(BF16)
        low = (mixed - high.astype(F32)).astype(BF16)
        pre = jnp.dot(high, weight[...], preferred_element_type=F32) + jnp.dot(
            low, weight[...], preferred_element_type=F32
        )
        sig = jax.nn.sigmoid(pre)
        if r == 0:
            activated[...] = (pre * sig).astype(BF16)
        act_grad = (cot[r].astype(F32) * sig * (1.0 + pre * (1.0 - sig))).astype(BF16)
        moved = lax.dot_general(
            act_grad, weight[...], (((1,), (1,)), ((), ())), preferred_element_type=F32
        ).astype(BF16)
        for part in (high, low):
            grad += lax.dot_general(
                part, act_grad, (((0,), (0,)), ((), ())), preferred_element_type=F32
            )
        for s in range(slots):
            term = jnp.dot(
                tile_cols[r, pl.ds(s * tile, tile), :], moved, preferred_element_type=F32
            )
            total[pos[r, s]] += term
    top = grad.astype(BF16)
    rest = (grad - top.astype(F32)).astype(BF16)
    ordered_top = jnp.dot(perm[...], top, preferred_element_type=F32).astype(BF16)
    ordered_rest = jnp.dot(perm[...], rest, preferred_element_type=F32).astype(BF16)
    share = blocks // len(NEAR)
    rows = perm.shape[0] // len(NEAR)
    for a, out in enumerate((out0, out1, out2, out3)):
        for k in range(share):
            out[pl.ds(k * tile, tile), :] = total[a * share + k].astype(BF16)
        out[pl.ds(share * tile, rows), :] = ordered_top[a * rows : (a + 1) * rows]
        out[pl.ds(share * tile + rows, rows), :] = ordered_rest[a * rows : (a + 1) * rows]


def shards(features, weight, tiles, tile_cols, tile_counts, cotangent):
    feat = features[0]
    tile = feat.shape[0]
    slots = tiles.shape[2]
    wide = lax.axis_size("wide")
    chips = wide // 2
    far = chips // CLASSES
    share = 2 * far
    w = lax.axis_index("wide")
    z, c = w // 2, w % 2
    sign = 1 - 2 * c

    def send(x, d):
        return lax.ppermute(
            x, "wide",
            [(2 * i + k, 2 * ((i + (d if k == 0 else -d)) % chips) + k) for i in range(chips) for k in range(2)],
        )

    def swap(x):
        return lax.ppermute(x, "wide", [(i, i ^ 1) for i in range(wide)])

    def every(step):
        return [
            [2 * (m + k) + core for m in range(0, chips, step)] for k in range(step) for core in range(2)
        ]

    with jax.named_scope("gather_far"):
        held = lax.all_gather(feat, "wide", axis_index_groups=every(2))
        held, tiles, cotangent, tile_cols, tile_counts = lax.optimization_barrier(
            (held, tiles, cotangent, tile_cols, tile_counts)
        )
    with jax.named_scope("gather_near"):
        beside = send(held, 1)
    with jax.named_scope("prepare"):
        rows = tiles[0].reshape(tile, slots * tile)
        both = jnp.concatenate([rows, cotangent[0]], axis=1)
        other = swap(both)
        tile_rows = jnp.stack([rows, other[:, : slots * tile]])
        tile_flip = jnp.swapaxes(tile_rows, 1, 2)
        cot = jnp.stack([cotangent[0], other[:, slots * tile :]])
        here = jnp.stack([w, w ^ 1])
        cols = tile_cols[0][here]
        counts = tile_counts[0][here]
        chip = cols // 2
        active = (jnp.arange(slots)[None, :] < counts[:, None]) & (cols % 2 == c)
        source = (z - chip) % 2 * (chips // 2) + chip // 2
        source = jnp.where(active, source, chips).astype(jnp.int32)
        offset = (sign * (z - chip)) % CLASSES
        place = offset % 4 * share + (offset + 1) // 4 % 2 * far + chip // CLASSES
        place = jnp.where(active, place, chips).astype(jnp.int32)
        spot = jnp.arange(chips)
        near_at = jnp.where(spot // share == 3, -1, spot // share)
        chip_at = (z - sign * (near_at + 4 * (spot % share // far))) % CLASSES + CLASSES * (spot % far)
        row_share = tile // wide
        row_at = ((2 * chip_at + c)[:, None] * row_share + jnp.arange(row_share)[None, :]).reshape(-1)
        perm = (row_at[:, None] == jnp.arange(tile)[None, :]).astype(BF16)
    mixed = pl.pallas_call(
        forward,
        out_shape=jax.ShapeDtypeStruct((2, tile, tile), F32),
        in_specs=[SMEM] + [VMEM] * 3,
        out_specs=VMEM,
        compiler_params=PARAMS,
        name="forward",
    )(source, held, beside, tile_rows)
    with jax.named_scope("pair"):
        theirs = swap(mixed)
    extra = share * row_share
    activated, *parts = pl.pallas_call(
        backward,
        out_shape=[jax.ShapeDtypeStruct((tile, tile), BF16)]
        + [jax.ShapeDtypeStruct((share * tile + 2 * extra, tile), BF16)] * len(NEAR),
        in_specs=[SMEM] + [VMEM] * 6,
        out_specs=[VMEM] * (1 + len(NEAR)),
        scratch_shapes=[pltpu.VMEM((chips + 1, tile, tile), F32)],
        compiler_params=PARAMS,
        name="backward",
    )(place, mixed, theirs, cot, tile_flip, weight, perm)
    def parted(whole, count):
        main = whole[: count * tile].astype(BF16)
        grad = whole[count * tile :]
        half = grad.shape[0] // 2
        grad = grad[:half] + grad[half:]
        top = grad.astype(BF16)
        return main, top, (grad - top.astype(F32)).astype(BF16)

    with jax.named_scope("scatter_near"):
        whole = parts[0].astype(F32)
        for part, d in zip(parts[1:], NEAR[1:]):
            whole += send(part, -d).astype(F32)
        pieces = parted(whole, share)
        keep, give = (
            jnp.concatenate([jnp.split(piece, 2)[half] for piece in pieces], 0) for half in range(2)
        )
    with jax.named_scope("scatter_middle"):
        whole = keep.astype(F32) + send(give, -4).astype(F32)
        pieces = parted(whole, far)
    with jax.named_scope("scatter_far"):
        message = jnp.concatenate([piece.reshape(far, -1, tile) for piece in pieces], 1)
        got = lax.all_to_all(message, "wide", 0, 0, axis_index_groups=every(CLASSES))
        whole = got.astype(F32).sum(0)
        feature_grad = whole[:tile].astype(BF16)
        grad = whole[tile : tile + row_share] + whole[tile + row_share :]
    with jax.named_scope("weight_sum"):
        groups = lax.axis_size("narrow")
        copies = lax.all_to_all(
            jnp.broadcast_to(grad[None], (groups, row_share, tile)), "narrow", 0, 0
        )
        weight_grad = copies.sum(0)
    return (activated[None], feature_grad[None], weight_grad)


def solution(mesh):
    placed = (
        P("narrow", "wide", None),
        P(),
        P("narrow", "wide", None, None),
        P("narrow", None, None),
        P("narrow", None),
        P("narrow", "wide", None),
    )
    return jax.shard_map(
        shards,
        mesh=mesh,
        in_specs=placed,
        out_specs=(P("narrow", "wide", None), P("narrow", "wide", None), P("wide", None)),
        check_vma=False,
    )
```

```python
import jax
import jax.numpy as jnp
from jax import lax
from jax.experimental import pallas as pl
from jax.experimental.pallas import tpu as pltpu
from jax.sharding import PartitionSpec as P

F32 = jnp.float32
BF16 = jnp.bfloat16
VMEM = pl.BlockSpec(memory_space=pltpu.VMEM)
SMEM = pl.BlockSpec(memory_space=pltpu.SMEM)
PARAMS = pltpu.CompilerParams(vmem_limit_bytes=32 * 1024 * 1024)

NEAR = (0, 1, 2, -1)
CLASSES = 4


def forward(pos, own, beside, rows_mine, rows_theirs, cot, out):
    slots = pos.shape[1]
    share = own.shape[0]
    for r, rows in enumerate((rows_mine, rows_theirs)):
        picked = []
        for s in range(slots):
            which, far = pos[r, s] // share, pos[r, s] % share
            block = jnp.zeros(own.shape[1:], BF16)
            block = jnp.where(which == 0, own[far], block)
            block = jnp.where(which == 1, beside[far], block)
            picked.append(block)
        out[r] = jnp.dot(rows[...], jnp.concatenate(picked, 0), preferred_element_type=F32)
    out[2] = cot[...].astype(F32)


def backward(
    pos, mine, theirs, cols_mine, cols_theirs, weight, perm,
    activated, out0, out1, out2, out3, total,
):
    slots = pos.shape[1]
    tile = weight.shape[0]
    blocks = total.shape[0] - 1
    total[...] = jnp.zeros_like(total)
    grad = jnp.zeros((tile, tile), F32)
    for r, (cols, cot) in enumerate(((cols_mine, mine), (cols_theirs, theirs))):
        mixed = mine[r] + theirs[1 - r]
        high = mixed.astype(BF16)
        low = (mixed - high.astype(F32)).astype(BF16)
        pre = jnp.dot(high, weight[...], preferred_element_type=F32) + jnp.dot(
            low, weight[...], preferred_element_type=F32
        )
        sig = jax.nn.sigmoid(pre)
        if r == 0:
            activated[...] = (pre * sig).astype(BF16)
        act_grad = (cot[2] * sig * (1.0 + pre * (1.0 - sig))).astype(BF16)
        moved = lax.dot_general(
            act_grad, weight[...], (((1,), (1,)), ((), ())), preferred_element_type=F32
        ).astype(BF16)
        for part in (high, low):
            grad += lax.dot_general(
                part, act_grad, (((0,), (0,)), ((), ())), preferred_element_type=F32
            )
        for s in range(slots):
            term = jnp.dot(
                cols[pl.ds(s * tile, tile), :], moved, preferred_element_type=F32
            )
            total[pos[r, s]] += term
    top = grad.astype(BF16)
    rest = (grad - top.astype(F32)).astype(BF16)
    ordered_top = jnp.dot(perm[...], top, preferred_element_type=F32).astype(BF16)
    ordered_rest = jnp.dot(perm[...], rest, preferred_element_type=F32).astype(BF16)
    share = blocks // CLASSES
    rows = perm.shape[0] // CLASSES
    for a, out in enumerate((out0, out1, out2, out3)):
        for k in range(share):
            out[pl.ds(k * tile, tile), :] = total[a * share + k].astype(BF16)
        out[pl.ds(share * tile, rows), :] = ordered_top[a * rows : (a + 1) * rows]
        out[pl.ds(share * tile + rows, rows), :] = ordered_rest[a * rows : (a + 1) * rows]


def shards(features, weight, tiles, tile_cols, tile_counts, cotangent):
    feat = features[0]
    tile = feat.shape[0]
    slots = tiles.shape[2]
    wide = lax.axis_size("wide")
    chips = wide // 2
    share = chips // CLASSES
    w = lax.axis_index("wide")
    z, c = w // 2, w % 2
    sign = 1 - 2 * c

    def send(x, d):
        return lax.ppermute(
            x, "wide",
            [(2 * i + k, 2 * ((i + (d if k == 0 else -d)) % chips) + k) for i in range(chips) for k in range(2)],
        )

    def swap(x):
        return lax.ppermute(x, "wide", [(i, i ^ 1) for i in range(wide)])

    def every(step):
        return [
            [2 * (m + k) + core for m in range(0, chips, step)] for k in range(step) for core in range(2)
        ]

    with jax.named_scope("gather_far"):
        other = swap(tiles)
        held = lax.all_gather(feat, "wide", axis_index_groups=every(2))
        held, tiles, other, tile_cols, tile_counts = lax.optimization_barrier(
            (held, tiles, other, tile_cols, tile_counts)
        )
    with jax.named_scope("gather_near"):
        beside = send(held, 1)
    with jax.named_scope("prepare"):
        rows = [t[0].reshape(tile, slots * tile) for t in (tiles, other)]
        flipped = [r.T for r in rows]
        here = jnp.stack([w, w ^ 1])
        cols = tile_cols[0][here]
        counts = tile_counts[0][here]
        chip = cols // 2
        active = (jnp.arange(slots)[None, :] < counts[:, None]) & (cols % 2 == c)
        source = (z - chip) % 2 * (chips // 2) + chip // 2
        source = jnp.where(active, source, chips).astype(jnp.int32)
        place = (sign * (z - chip)) % CLASSES * share + chip // CLASSES
        place = jnp.where(active, place, chips).astype(jnp.int32)
        spot = jnp.arange(chips)
        chip_at = (z - sign * (spot // share)) % CLASSES + CLASSES * (spot % share)
        row_share = tile // wide
        row_at = ((2 * chip_at + c)[:, None] * row_share + jnp.arange(row_share)[None, :]).reshape(-1)
        perm = (row_at[:, None] == jnp.arange(tile)[None, :]).astype(BF16)
    mixed = pl.pallas_call(
        forward,
        out_shape=jax.ShapeDtypeStruct((3, tile, tile), F32),
        in_specs=[SMEM] + [VMEM] * 5,
        out_specs=VMEM,
        compiler_params=PARAMS,
        name="forward",
    )(source, held, beside, *rows, cotangent[0])
    with jax.named_scope("pair"):
        theirs = swap(mixed)
    extra = share * row_share
    activated, *parts = pl.pallas_call(
        backward,
        out_shape=[jax.ShapeDtypeStruct((tile, tile), BF16)]
        + [jax.ShapeDtypeStruct((share * tile + 2 * extra, tile), BF16)] * CLASSES,
        in_specs=[SMEM] + [VMEM] * 6,
        out_specs=[VMEM] * (1 + CLASSES),
        scratch_shapes=[pltpu.VMEM((chips + 1, tile, tile), F32)],
        compiler_params=PARAMS,
        name="backward",
    )(place, mixed, theirs, *flipped, weight, perm)
    with jax.named_scope("scatter_near"):
        whole = parts[0].astype(F32)
        for part, d in zip(parts[1:], NEAR[1:]):
            whole += send(part, -d).astype(F32)
        main = whole[: share * tile].reshape(share, tile, tile).astype(BF16)
        grad = whole[share * tile : share * tile + extra] + whole[share * tile + extra :]
        grad = grad.reshape(share, row_share, tile)
    with jax.named_scope("scatter_far"):
        top = grad.astype(BF16)
        rest = (grad - top.astype(F32)).astype(BF16)
        message = jnp.concatenate([main, top, rest], 1)
        got = lax.all_to_all(message, "wide", 0, 0, axis_index_groups=every(CLASSES))
        whole = got.astype(F32).sum(0)
        feature_grad = whole[:tile].astype(BF16)
        grad = whole[tile : tile + row_share] + whole[tile + row_share :]
    with jax.named_scope("weight_sum"):
        groups = lax.axis_size("narrow")
        copies = lax.all_to_all(
            jnp.broadcast_to(grad[None], (groups, row_share, tile)), "narrow", 0, 0
        )
        weight_grad = copies.sum(0)
    return (activated[None], feature_grad[None], weight_grad)


def solution(mesh):
    placed = (
        P("narrow", "wide", None),
        P(),
        P("narrow", "wide", None, None),
        P("narrow", None, None),
        P("narrow", None),
        P("narrow", "wide", None),
    )
    return jax.shard_map(
        shards,
        mesh=mesh,
        in_specs=placed,
        out_specs=(P("narrow", "wide", None), P("narrow", "wide", None), P("wide", None)),
        check_vma=False,
    )
```

```python
import jax
import jax.numpy as jnp
from jax import lax
from jax.experimental import pallas as pl
from jax.experimental.pallas import tpu as pltpu
from jax.sharding import PartitionSpec as P

F32 = jnp.float32
BF16 = jnp.bfloat16
VMEM = pl.BlockSpec(memory_space=pltpu.VMEM)
SMEM = pl.BlockSpec(memory_space=pltpu.SMEM)
PARAMS = pltpu.CompilerParams(vmem_limit_bytes=32 * 1024 * 1024)

NEAR = (0, 1, 2, -1)
CLASSES = 4


def forward(pos, own, beside, rows_mine, rows_theirs, cot, out):
    slots = pos.shape[1]
    share = own.shape[0]
    for r, rows in enumerate((rows_mine, rows_theirs)):
        picked = []
        for s in range(slots):
            which, far = pos[r, s] // share, pos[r, s] % share
            block = jnp.zeros(own.shape[1:], BF16)
            block = jnp.where(which == 0, own[far], block)
            block = jnp.where(which == 1, beside[far], block)
            picked.append(block)
        out[r] = jnp.dot(rows[...], jnp.concatenate(picked, 0), preferred_element_type=F32)
    out[2] = cot[...].astype(F32)


def backward(
    pos, mine, theirs, cols_mine, cols_theirs, weight, perm,
    activated, out0, out1, out2, out3, total,
):
    slots = pos.shape[1]
    tile = weight.shape[0]
    blocks = total.shape[0] - 1
    total[...] = jnp.zeros_like(total)
    grad = jnp.zeros((tile, tile), F32)
    for r, (cols, cot) in enumerate(((cols_mine, mine), (cols_theirs, theirs))):
        mixed = mine[r] + theirs[1 - r]
        high = mixed.astype(BF16)
        low = (mixed - high.astype(F32)).astype(BF16)
        pre = jnp.dot(high, weight[...], preferred_element_type=F32) + jnp.dot(
            low, weight[...], preferred_element_type=F32
        )
        sig = jax.nn.sigmoid(pre)
        if r == 0:
            activated[...] = (pre * sig).astype(BF16)
        act_grad = (cot[2] * sig * (1.0 + pre * (1.0 - sig))).astype(BF16)
        moved = lax.dot_general(
            act_grad, weight[...], (((1,), (1,)), ((), ())), preferred_element_type=F32
        ).astype(BF16)
        for part in (high, low):
            grad += lax.dot_general(
                part, act_grad, (((0,), (0,)), ((), ())), preferred_element_type=F32
            )
        for s in range(slots):
            term = jnp.dot(
                cols[pl.ds(s * tile, tile), :], moved, preferred_element_type=F32
            )
            total[pos[r, s]] += term
    top = grad.astype(BF16)
    rest = (grad - top.astype(F32)).astype(BF16)
    ordered_top = jnp.dot(perm[...], top, preferred_element_type=F32).astype(BF16)
    ordered_rest = jnp.dot(perm[...], rest, preferred_element_type=F32).astype(BF16)
    share = blocks // CLASSES
    rows = perm.shape[0] // CLASSES
    for a, out in enumerate((out0, out1, out2, out3)):
        for k in range(share):
            out[pl.ds(k * tile, tile), :] = total[a * share + k].astype(BF16)
        out[pl.ds(share * tile, rows), :] = ordered_top[a * rows : (a + 1) * rows]
        out[pl.ds(share * tile + rows, rows), :] = ordered_rest[a * rows : (a + 1) * rows]


def shards(features, weight, tiles, tile_cols, tile_counts, cotangent):
    feat = features[0]
    tile = feat.shape[0]
    slots = tiles.shape[2]
    wide = lax.axis_size("wide")
    chips = wide // 2
    share = chips // CLASSES
    w = lax.axis_index("wide")
    z, c = w // 2, w % 2
    sign = 1 - 2 * c

    def send(x, d):
        return lax.ppermute(
            x, "wide",
            [(2 * i + k, 2 * ((i + (d if k == 0 else -d)) % chips) + k) for i in range(chips) for k in range(2)],
        )

    def swap(x):
        return lax.ppermute(x, "wide", [(i, i ^ 1) for i in range(wide)])

    def every(step):
        return [
            [2 * (m + k) + core for m in range(0, chips, step)][:: 1 - 2 * core]
            for k in range(step) for core in range(2)
        ]

    def order(chip, step):
        return jnp.where(c == 0, chip // step, chips // step - 1 - chip // step)

    with jax.named_scope("gather_far"):
        other = swap(tiles)
        held = lax.all_gather(feat, "wide", axis_index_groups=every(2))
        held, tiles, other, tile_cols, tile_counts = lax.optimization_barrier(
            (held, tiles, other, tile_cols, tile_counts)
        )
    with jax.named_scope("gather_near"):
        beside = send(held, 1)
    with jax.named_scope("prepare"):
        rows = [t[0].reshape(tile, slots * tile) for t in (tiles, other)]
        flipped = [r.T for r in rows]
        here = jnp.stack([w, w ^ 1])
        cols = tile_cols[0][here]
        counts = tile_counts[0][here]
        chip = cols // 2
        active = (jnp.arange(slots)[None, :] < counts[:, None]) & (cols % 2 == c)
        source = (z - chip) % 2 * (chips // 2) + order(chip, 2)
        source = jnp.where(active, source, chips).astype(jnp.int32)
        place = (sign * (z - chip)) % CLASSES * share + order(chip, CLASSES)
        place = jnp.where(active, place, chips).astype(jnp.int32)
        spot = jnp.arange(chips)
        chip_at = (z - sign * (spot // share)) % CLASSES + CLASSES * order(CLASSES * (spot % share), CLASSES)
        row_share = tile // wide
        row_at = ((2 * chip_at + c)[:, None] * row_share + jnp.arange(row_share)[None, :]).reshape(-1)
        perm = (row_at[:, None] == jnp.arange(tile)[None, :]).astype(BF16)
    mixed = pl.pallas_call(
        forward,
        out_shape=jax.ShapeDtypeStruct((3, tile, tile), F32),
        in_specs=[SMEM] + [VMEM] * 5,
        out_specs=VMEM,
        compiler_params=PARAMS,
        name="forward",
    )(source, held, beside, *rows, cotangent[0])
    with jax.named_scope("pair"):
        theirs = swap(mixed)
    extra = share * row_share
    activated, *parts = pl.pallas_call(
        backward,
        out_shape=[jax.ShapeDtypeStruct((tile, tile), BF16)]
        + [jax.ShapeDtypeStruct((share * tile + 2 * extra, tile), BF16)] * CLASSES,
        in_specs=[SMEM] + [VMEM] * 6,
        out_specs=[VMEM] * (1 + CLASSES),
        scratch_shapes=[pltpu.VMEM((chips + 1, tile, tile), F32)],
        compiler_params=PARAMS,
        name="backward",
    )(place, mixed, theirs, *flipped, weight, perm)
    with jax.named_scope("scatter_near"):
        whole = parts[0].astype(F32)
        for part, d in zip(parts[1:], NEAR[1:]):
            whole += send(part, -d).astype(F32)
        main = whole[: share * tile].reshape(share, tile, tile).astype(BF16)
        grad = whole[share * tile : share * tile + extra] + whole[share * tile + extra :]
        grad = grad.reshape(share, row_share, tile)
    with jax.named_scope("scatter_far"):
        top = grad.astype(BF16)
        rest = (grad - top.astype(F32)).astype(BF16)
        message = jnp.concatenate([main, top, rest], 1)
        got = lax.all_to_all(message, "wide", 0, 0, axis_index_groups=every(CLASSES))
        whole = got.astype(F32).sum(0)
        feature_grad = whole[:tile].astype(BF16)
        grad = whole[tile : tile + row_share] + whole[tile + row_share :]
    with jax.named_scope("weight_sum"):
        groups = lax.axis_size("narrow")
        copies = lax.all_to_all(
            jnp.broadcast_to(grad[None], (groups, row_share, tile)), "narrow", 0, 0
        )
        weight_grad = copies.sum(0)
    return (activated[None], feature_grad[None], weight_grad)


def solution(mesh):
    placed = (
        P("narrow", "wide", None),
        P(),
        P("narrow", "wide", None, None),
        P("narrow", None, None),
        P("narrow", None),
        P("narrow", "wide", None),
    )
    return jax.shard_map(
        shards,
        mesh=mesh,
        in_specs=placed,
        out_specs=(P("narrow", "wide", None), P("narrow", "wide", None), P("wide", None)),
        check_vma=False,
    )
```

```python
import jax
import jax.numpy as jnp
from jax import lax
from jax.experimental import pallas as pl
from jax.experimental.pallas import tpu as pltpu
from jax.sharding import PartitionSpec as P

F32 = jnp.float32
BF16 = jnp.bfloat16
VMEM = pl.BlockSpec(memory_space=pltpu.VMEM)
SMEM = pl.BlockSpec(memory_space=pltpu.SMEM)
PARAMS = pltpu.CompilerParams(vmem_limit_bytes=32 * 1024 * 1024)

NEAR = (0, 1, 2, -1)
CLASSES = 4


def forward(pos, own, beside, rows_mine, rows_theirs, cot, out):
    slots = pos.shape[1]
    share = own.shape[0]
    for r, rows in enumerate((rows_mine, rows_theirs)):
        picked = []
        for s in range(slots):
            which, far = pos[r, s] // share, pos[r, s] % share
            block = jnp.zeros(own.shape[1:], BF16)
            block = jnp.where(which == 0, own[far], block)
            block = jnp.where(which == 1, beside[far], block)
            picked.append(block)
        out[r] = jnp.dot(rows[...], jnp.concatenate(picked, 0), preferred_element_type=F32)
    out[2] = cot[...].astype(F32)


def backward(
    pos, mine, theirs, cols_mine, cols_theirs, weight, perm,
    activated, out0, out1, out2, out3, total,
):
    slots = pos.shape[1]
    tile = weight.shape[0]
    blocks = total.shape[0] - 1
    total[...] = jnp.zeros_like(total)
    grad = jnp.zeros((tile, tile), F32)
    for r, (cols, cot) in enumerate(((cols_mine, mine), (cols_theirs, theirs))):
        mixed = mine[r] + theirs[1 - r]
        high = mixed.astype(BF16)
        low = (mixed - high.astype(F32)).astype(BF16)
        pre = jnp.dot(high, weight[...], preferred_element_type=F32) + jnp.dot(
            low, weight[...], preferred_element_type=F32
        )
        sig = jax.nn.sigmoid(pre)
        if r == 0:
            activated[...] = (pre * sig).astype(BF16)
        act_grad = (cot[2] * sig * (1.0 + pre * (1.0 - sig))).astype(BF16)
        moved = lax.dot_general(
            act_grad, weight[...], (((1,), (1,)), ((), ())), preferred_element_type=F32
        ).astype(BF16)
        for part in (high, low):
            grad += lax.dot_general(
                part, act_grad, (((0,), (0,)), ((), ())), preferred_element_type=F32
            )
        for s in range(slots):
            term = jnp.dot(
                cols[pl.ds(s * tile, tile), :], moved, preferred_element_type=F32
            )
            total[pos[r, s]] += term
    top = grad.astype(BF16)
    rest = (grad - top.astype(F32)).astype(BF16)
    ordered_top = jnp.dot(perm[...], top, preferred_element_type=F32).astype(BF16)
    ordered_rest = jnp.dot(perm[...], rest, preferred_element_type=F32).astype(BF16)
    share = blocks // CLASSES
    rows = perm.shape[0] // CLASSES
    for a, out in enumerate((out0, out1, out2, out3)):
        for k in range(share):
            out[pl.ds(k * tile, tile), :] = total[a * share + k].astype(BF16)
        out[pl.ds(share * tile, rows), :] = ordered_top[a * rows : (a + 1) * rows]
        out[pl.ds(share * tile + rows, rows), :] = ordered_rest[a * rows : (a + 1) * rows]


def shards(features, weight, tiles, tile_cols, tile_counts, cotangent):
    feat = features[0]
    tile = feat.shape[0]
    slots = tiles.shape[2]
    wide = lax.axis_size("wide")
    chips = wide // 2
    share = chips // CLASSES
    w = lax.axis_index("wide")
    z, c = w // 2, w % 2
    sign = 1 - 2 * c

    def send(x, d):
        return lax.ppermute(
            x, "wide",
            [(2 * i + k, 2 * ((i + (d if k == 0 else -d)) % chips) + k) for i in range(chips) for k in range(2)],
        )

    def swap(x):
        return lax.ppermute(x, "wide", [(i, i ^ 1) for i in range(wide)])

    def every(step):
        return [
            [2 * (m + k) + core for m in range(0, chips, step)] for k in range(step) for core in range(2)
        ]

    with jax.named_scope("gather_far"):
        held = lax.all_gather(feat, "wide", axis_index_groups=every(2))
    with jax.named_scope("gather_near"):
        beside = send(held, 1)
    with jax.named_scope("prepare"):
        after = lax.optimization_barrier(held[0, :8] + held[-1, :8])
        _, tiles, tile_cols, tile_counts = lax.optimization_barrier((after, tiles, tile_cols, tile_counts))
        other = swap(tiles)
        rows = [t[0].reshape(tile, slots * tile) for t in (tiles, other)]
        flipped = [r.T for r in rows]
        here = jnp.stack([w, w ^ 1])
        cols = tile_cols[0][here]
        counts = tile_counts[0][here]
        chip = cols // 2
        active = (jnp.arange(slots)[None, :] < counts[:, None]) & (cols % 2 == c)
        source = (z - chip) % 2 * (chips // 2) + chip // 2
        source = jnp.where(active, source, chips).astype(jnp.int32)
        place = (sign * (z - chip)) % CLASSES * share + chip // CLASSES
        place = jnp.where(active, place, chips).astype(jnp.int32)
        spot = jnp.arange(chips)
        chip_at = (z - sign * (spot // share)) % CLASSES + CLASSES * (spot % share)
        row_share = tile // wide
        row_at = ((2 * chip_at + c)[:, None] * row_share + jnp.arange(row_share)[None, :]).reshape(-1)
        perm = (row_at[:, None] == jnp.arange(tile)[None, :]).astype(BF16)
    mixed = pl.pallas_call(
        forward,
        out_shape=jax.ShapeDtypeStruct((3, tile, tile), F32),
        in_specs=[SMEM] + [VMEM] * 5,
        out_specs=VMEM,
        compiler_params=PARAMS,
        name="forward",
    )(source, held, beside, *rows, cotangent[0])
    with jax.named_scope("pair"):
        theirs = swap(mixed)
    extra = share * row_share
    activated, *parts = pl.pallas_call(
        backward,
        out_shape=[jax.ShapeDtypeStruct((tile, tile), BF16)]
        + [jax.ShapeDtypeStruct((share * tile + 2 * extra, tile), BF16)] * CLASSES,
        in_specs=[SMEM] + [VMEM] * 6,
        out_specs=[VMEM] * (1 + CLASSES),
        scratch_shapes=[pltpu.VMEM((chips + 1, tile, tile), F32)],
        compiler_params=PARAMS,
        name="backward",
    )(place, mixed, theirs, *flipped, weight, perm)
    with jax.named_scope("scatter_near"):
        whole = parts[0].astype(F32)
        for part, d in zip(parts[1:], NEAR[1:]):
            whole += send(part, -d).astype(F32)
        main = whole[: share * tile].reshape(share, tile, tile).astype(BF16)
        grad = whole[share * tile : share * tile + extra] + whole[share * tile + extra :]
        grad = grad.reshape(share, row_share, tile)
    with jax.named_scope("scatter_far"):
        top = grad.astype(BF16)
        rest = (grad - top.astype(F32)).astype(BF16)
        message = jnp.concatenate([main, top, rest], 1)
        got = lax.all_to_all(message, "wide", 0, 0, axis_index_groups=every(CLASSES))
        whole = got.astype(F32).sum(0)
        feature_grad = whole[:tile].astype(BF16)
        grad = whole[tile : tile + row_share] + whole[tile + row_share :]
    with jax.named_scope("weight_sum"):
        groups = lax.axis_size("narrow")
        copies = lax.all_to_all(
            jnp.broadcast_to(grad[None], (groups, row_share, tile)), "narrow", 0, 0
        )
        weight_grad = copies.sum(0)
    return (activated[None], feature_grad[None], weight_grad)


def solution(mesh):
    placed = (
        P("narrow", "wide", None),
        P(),
        P("narrow", "wide", None, None),
        P("narrow", None, None),
        P("narrow", None),
        P("narrow", "wide", None),
    )
    return jax.shard_map(
        shards,
        mesh=mesh,
        in_specs=placed,
        out_specs=(P("narrow", "wide", None), P("narrow", "wide", None), P("wide", None)),
        check_vma=False,
    )
```

```python
import jax
import jax.numpy as jnp
from jax import lax
from jax.experimental import pallas as pl
from jax.experimental.pallas import tpu as pltpu
from jax.sharding import PartitionSpec as P

F32 = jnp.float32
BF16 = jnp.bfloat16
VMEM = pl.BlockSpec(memory_space=pltpu.VMEM)
SMEM = pl.BlockSpec(memory_space=pltpu.SMEM)
PARAMS = pltpu.CompilerParams(vmem_limit_bytes=32 * 1024 * 1024)

NEAR = (0, 1, 2, -1)
CLASSES = 4


def forward(pos, own, beside, rows_mine, rows_theirs, cot, out):
    slots = pos.shape[1]
    share = own.shape[0]
    for r, rows in enumerate((rows_mine, rows_theirs)):
        picked = []
        for s in range(slots):
            which, far = pos[r, s] // share, pos[r, s] % share
            block = jnp.zeros(own.shape[1:], BF16)
            block = jnp.where(which == 0, own[far], block)
            block = jnp.where(which == 1, beside[far], block)
            picked.append(block)
        out[r] = jnp.dot(rows[...], jnp.concatenate(picked, 0), preferred_element_type=F32)
    out[2] = cot[...].astype(F32)


def backward(
    pos, mine, theirs, cols_mine, cols_theirs, weight, perm,
    activated, ordered, out0, out1, out2, out3, total,
):
    slots = pos.shape[1]
    tile = weight.shape[0]
    blocks = total.shape[0] - 1
    total[...] = jnp.zeros_like(total)
    grad = jnp.zeros((tile, tile), F32)
    for r, (cols, cot) in enumerate(((cols_mine, mine), (cols_theirs, theirs))):
        mixed = mine[r] + theirs[1 - r]
        high = mixed.astype(BF16)
        low = (mixed - high.astype(F32)).astype(BF16)
        pre = jnp.dot(high, weight[...], preferred_element_type=F32) + jnp.dot(
            low, weight[...], preferred_element_type=F32
        )
        sig = jax.nn.sigmoid(pre)
        if r == 0:
            activated[...] = (pre * sig).astype(BF16)
        act_grad = (cot[2] * sig * (1.0 + pre * (1.0 - sig))).astype(BF16)
        moved = lax.dot_general(
            act_grad, weight[...], (((1,), (1,)), ((), ())), preferred_element_type=F32
        ).astype(BF16)
        for part in (high, low):
            grad += lax.dot_general(
                part, act_grad, (((0,), (0,)), ((), ())), preferred_element_type=F32
            )
        for s in range(slots):
            term = jnp.dot(
                cols[pl.ds(s * tile, tile), :], moved, preferred_element_type=F32
            )
            total[pos[r, s]] += term
    top = grad.astype(BF16)
    rest = (grad - top.astype(F32)).astype(BF16)
    ordered[...] = jnp.dot(perm[...], top, preferred_element_type=F32) + jnp.dot(
        perm[...], rest, preferred_element_type=F32
    )
    share = blocks // CLASSES
    for a, out in enumerate((out0, out1, out2, out3)):
        for k in range(share):
            out[k] = total[a * share + k].astype(BF16)


def shards(features, weight, tiles, tile_cols, tile_counts, cotangent):
    feat = features[0]
    tile = feat.shape[0]
    slots = tiles.shape[2]
    wide = lax.axis_size("wide")
    chips = wide // 2
    share = chips // CLASSES
    w = lax.axis_index("wide")
    z, c = w // 2, w % 2
    sign = 1 - 2 * c

    def send(x, d):
        return lax.ppermute(
            x, "wide",
            [(2 * i + k, 2 * ((i + (d if k == 0 else -d)) % chips) + k) for i in range(chips) for k in range(2)],
        )

    def swap(x):
        return lax.ppermute(x, "wide", [(i, i ^ 1) for i in range(wide)])

    def every(step):
        return [
            [2 * (m + k) + core for m in range(0, chips, step)] for k in range(step) for core in range(2)
        ]

    with jax.named_scope("gather_far"):
        held = lax.all_gather(feat, "wide", axis_index_groups=every(2))
    with jax.named_scope("gather_near"):
        beside = send(held, 1)
    with jax.named_scope("prepare"):
        after = lax.optimization_barrier(held[0, :8] + held[-1, :8])
        _, tiles, tile_cols, tile_counts = lax.optimization_barrier((after, tiles, tile_cols, tile_counts))
        other = swap(tiles)
        rows = [t[0].reshape(tile, slots * tile) for t in (tiles, other)]
        flipped = [r.T for r in rows]
        here = jnp.stack([w, w ^ 1])
        cols = tile_cols[0][here]
        counts = tile_counts[0][here]
        chip = cols // 2
        active = (jnp.arange(slots)[None, :] < counts[:, None]) & (cols % 2 == c)
        source = (z - chip) % 2 * (chips // 2) + chip // 2
        source = jnp.where(active, source, chips).astype(jnp.int32)
        place = (sign * (z - chip)) % CLASSES * share + chip // CLASSES
        place = jnp.where(active, place, chips).astype(jnp.int32)
        spot = jnp.arange(chips)
        chip_at = (z - sign * (spot // share)) % CLASSES + CLASSES * (spot % share)
        row_share = tile // wide
        row_at = ((2 * chip_at + c)[:, None] * row_share + jnp.arange(row_share)[None, :]).reshape(-1)
        perm = (row_at[:, None] == jnp.arange(tile)[None, :]).astype(BF16)
    mixed = pl.pallas_call(
        forward,
        out_shape=jax.ShapeDtypeStruct((3, tile, tile), F32),
        in_specs=[SMEM] + [VMEM] * 5,
        out_specs=VMEM,
        compiler_params=PARAMS,
        name="forward",
    )(source, held, beside, *rows, cotangent[0])
    with jax.named_scope("pair"):
        theirs = swap(mixed)
    activated, grad, *parts = pl.pallas_call(
        backward,
        out_shape=[
            jax.ShapeDtypeStruct((tile, tile), BF16),
            jax.ShapeDtypeStruct((tile // 2, tile), F32),
        ]
        + [jax.ShapeDtypeStruct((share, tile, tile), BF16)] * CLASSES,
        in_specs=[SMEM] + [VMEM] * 6,
        out_specs=[VMEM] * (2 + CLASSES),
        scratch_shapes=[pltpu.VMEM((chips + 1, tile, tile), F32)],
        compiler_params=PARAMS,
        name="backward",
    )(place, mixed, theirs, *flipped, weight, perm)
    with jax.named_scope("weight_groups"):
        groups = lax.axis_size("narrow")
        grad = lax.all_to_all(jnp.broadcast_to(grad[None], (groups,) + grad.shape), "narrow", 0, 0).sum(0)
        grads = grad.reshape(CLASSES, share, row_share, tile)
    with jax.named_scope("scatter_near"):
        whole = parts[0].astype(F32)
        for part, d in zip(parts[1:], NEAR[1:]):
            whole += send(part, -d).astype(F32)
        main = whole.astype(BF16)
    with jax.named_scope("weight_near"):
        grad = grads[0]
        for a, d in list(enumerate(NEAR))[1:]:
            grad += send(grads[a], -d)
    with jax.named_scope("scatter_far"):
        top = grad.astype(BF16)
        rest = (grad - top.astype(F32)).astype(BF16)
        message = jnp.concatenate([main, top, rest], 1)
        got = lax.all_to_all(message, "wide", 0, 0, axis_index_groups=every(CLASSES))
        whole = got.astype(F32).sum(0)
        feature_grad = whole[:tile].astype(BF16)
        weight_grad = whole[tile : tile + row_share] + whole[tile + row_share :]
    return (activated[None], feature_grad[None], weight_grad)


def solution(mesh):
    placed = (
        P("narrow", "wide", None),
        P(),
        P("narrow", "wide", None, None),
        P("narrow", None, None),
        P("narrow", None),
        P("narrow", "wide", None),
    )
    return jax.shard_map(
        shards,
        mesh=mesh,
        in_specs=placed,
        out_specs=(P("narrow", "wide", None), P("narrow", "wide", None), P("wide", None)),
        check_vma=False,
    )
```

```python
import jax
import jax.numpy as jnp
from jax import lax
from jax.experimental import pallas as pl
from jax.experimental.pallas import tpu as pltpu
from jax.sharding import PartitionSpec as P

F32 = jnp.float32
BF16 = jnp.bfloat16
VMEM = pl.BlockSpec(memory_space=pltpu.VMEM)
SMEM = pl.BlockSpec(memory_space=pltpu.SMEM)
PARAMS = pltpu.CompilerParams(vmem_limit_bytes=32 * 1024 * 1024)

NEAR = (0, 1, 2, -1)
CLASSES = 4


def forward(pos, own, beside, rows_mine, rows_theirs, cot, out):
    slots = pos.shape[1]
    share = own.shape[0]
    for r, rows in enumerate((rows_mine, rows_theirs)):
        picked = []
        for s in range(slots):
            which, far = pos[r, s] // share, pos[r, s] % share
            block = jnp.zeros(own.shape[1:], BF16)
            block = jnp.where(which == 0, own[far], block)
            block = jnp.where(which == 1, beside[far], block)
            picked.append(block)
        out[r] = jnp.dot(rows[...], jnp.concatenate(picked, 0), preferred_element_type=F32)
    out[2] = cot[...].astype(F32)


def backward(
    pos, mine, theirs, cols_mine, cols_theirs, weight, perm,
    activated, ordered, out0, out1, out2, out3, total,
):
    slots = pos.shape[1]
    tile = weight.shape[0]
    blocks = total.shape[0] - 1
    total[...] = jnp.zeros_like(total)
    grad = jnp.zeros((tile, tile), F32)
    for r, (cols, cot) in enumerate(((cols_mine, mine), (cols_theirs, theirs))):
        mixed = mine[r] + theirs[1 - r]
        high = mixed.astype(BF16)
        low = (mixed - high.astype(F32)).astype(BF16)
        pre = jnp.dot(high, weight[...], preferred_element_type=F32) + jnp.dot(
            low, weight[...], preferred_element_type=F32
        )
        sig = jax.nn.sigmoid(pre)
        if r == 0:
            activated[...] = (pre * sig).astype(BF16)
        act_grad = (cot[2] * sig * (1.0 + pre * (1.0 - sig))).astype(BF16)
        moved = lax.dot_general(
            act_grad, weight[...], (((1,), (1,)), ((), ())), preferred_element_type=F32
        ).astype(BF16)
        for part in (high, low):
            grad += lax.dot_general(
                part, act_grad, (((0,), (0,)), ((), ())), preferred_element_type=F32
            )
        for s in range(slots):
            term = jnp.dot(
                cols[pl.ds(s * tile, tile), :], moved, preferred_element_type=F32
            )
            total[pos[r, s]] += term
    top = grad.astype(BF16)
    rest = (grad - top.astype(F32)).astype(BF16)
    ordered[...] = jnp.dot(perm[...], top, preferred_element_type=F32) + jnp.dot(
        perm[...], rest, preferred_element_type=F32
    )
    share = blocks // CLASSES
    for a, out in enumerate((out0, out1, out2, out3)):
        for k in range(share):
            out[k] = total[a * share + k].astype(BF16)


def shards(features, weight, tiles, tile_cols, tile_counts, cotangent):
    feat = features[0]
    tile = feat.shape[0]
    slots = tiles.shape[2]
    wide = lax.axis_size("wide")
    chips = wide // 2
    share = chips // CLASSES
    w = lax.axis_index("wide")
    z, c = w // 2, w % 2
    sign = 1 - 2 * c

    def send(x, d):
        return lax.ppermute(
            x, "wide",
            [(2 * i + k, 2 * ((i + (d if k == 0 else -d)) % chips) + k) for i in range(chips) for k in range(2)],
        )

    def swap(x):
        return lax.ppermute(x, "wide", [(i, i ^ 1) for i in range(wide)])

    def every(step):
        return [
            [2 * (m + k) + core for m in range(0, chips, step)] for k in range(step) for core in range(2)
        ]

    with jax.named_scope("gather_far"):
        held = lax.all_gather(feat, "wide", axis_index_groups=every(2))
    with jax.named_scope("gather_near"):
        beside = send(held, 1)
    with jax.named_scope("prepare"):
        after = lax.optimization_barrier(held[0, :8] + held[-1, :8])
        _, tiles, tile_cols, tile_counts = lax.optimization_barrier((after, tiles, tile_cols, tile_counts))
        other = swap(tiles)
        rows = [t[0].reshape(tile, slots * tile) for t in (tiles, other)]
        flipped = [r.T for r in rows]
        here = jnp.stack([w, w ^ 1])
        cols = tile_cols[0][here]
        counts = tile_counts[0][here]
        chip = cols // 2
        active = (jnp.arange(slots)[None, :] < counts[:, None]) & (cols % 2 == c)
        source = (z - chip) % 2 * (chips // 2) + chip // 2
        source = jnp.where(active, source, chips).astype(jnp.int32)
        place = (sign * (z - chip)) % CLASSES * share + chip // CLASSES
        place = jnp.where(active, place, chips).astype(jnp.int32)
        spot = jnp.arange(chips)
        chip_at = (z - sign * (spot // share)) % CLASSES + CLASSES * (spot % share)
        row_share = tile // wide
        row_at = ((2 * chip_at + c)[:, None] * row_share + jnp.arange(row_share)[None, :]).reshape(-1)
        perm = (row_at[:, None] == jnp.arange(tile)[None, :]).astype(BF16)
    mixed = pl.pallas_call(
        forward,
        out_shape=jax.ShapeDtypeStruct((3, tile, tile), F32),
        in_specs=[SMEM] + [VMEM] * 5,
        out_specs=VMEM,
        compiler_params=PARAMS,
        name="forward",
    )(source, held, beside, *rows, cotangent[0])
    with jax.named_scope("pair"):
        theirs = swap(mixed)
    activated, grad, *parts = pl.pallas_call(
        backward,
        out_shape=[
            jax.ShapeDtypeStruct((tile, tile), BF16),
            jax.ShapeDtypeStruct((tile // 2, tile), F32),
        ]
        + [jax.ShapeDtypeStruct((share, tile, tile), BF16)] * CLASSES,
        in_specs=[SMEM] + [VMEM] * 6,
        out_specs=[VMEM] * (2 + CLASSES),
        scratch_shapes=[pltpu.VMEM((chips + 1, tile, tile), F32)],
        compiler_params=PARAMS,
        name="backward",
    )(place, mixed, theirs, *flipped, weight, perm)
    with jax.named_scope("weight_groups"):
        groups = lax.axis_size("narrow")
        grad = lax.all_to_all(jnp.broadcast_to(grad[None], (groups,) + grad.shape), "narrow", 0, 0).sum(0)
        grads = grad.reshape(CLASSES, share, row_share, tile)
    def split(x):
        top = x.astype(BF16)
        return [top, (x - top.astype(F32)).astype(BF16)]

    def joined(x):
        return x[:, :tile], x[:, tile : tile + row_share] + x[:, tile + row_share :]

    with jax.named_scope("scatter_near"):
        both = send(jnp.concatenate([parts[1], *split(grads[1])], 1), -NEAR[1])
        near_main, near_grad = joined(both.astype(F32))
        whole = parts[0].astype(F32) + near_main
        grad = grads[0] + near_grad
        for a in (2, 3):
            whole += send(parts[a], -NEAR[a]).astype(F32)
            grad += send(grads[a], -NEAR[a])
    with jax.named_scope("scatter_far"):
        message = jnp.concatenate([whole.astype(BF16), *split(grad)], 1)
        got = lax.all_to_all(message, "wide", 0, 0, axis_index_groups=every(CLASSES))
        whole = got.astype(F32).sum(0)
        feature_grad = whole[:tile].astype(BF16)
        weight_grad = whole[tile : tile + row_share] + whole[tile + row_share :]
    return (activated[None], feature_grad[None], weight_grad)


def solution(mesh):
    placed = (
        P("narrow", "wide", None),
        P(),
        P("narrow", "wide", None, None),
        P("narrow", None, None),
        P("narrow", None),
        P("narrow", "wide", None),
    )
    return jax.shard_map(
        shards,
        mesh=mesh,
        in_specs=placed,
        out_specs=(P("narrow", "wide", None), P("narrow", "wide", None), P("wide", None)),
        check_vma=False,
    )
```

```python
import jax
import jax.numpy as jnp
from jax import lax
from jax.experimental import pallas as pl
from jax.experimental.pallas import tpu as pltpu
from jax.sharding import PartitionSpec as P

F32 = jnp.float32
BF16 = jnp.bfloat16
VMEM = pl.BlockSpec(memory_space=pltpu.VMEM)
SMEM = pl.BlockSpec(memory_space=pltpu.SMEM)
PARAMS = pltpu.CompilerParams(vmem_limit_bytes=32 * 1024 * 1024)

NEAR = (0, 1, 2, -1)
CLASSES = 4


def forward(pos, own, beside, rows_mine, rows_theirs, cot, out):
    slots = pos.shape[1]
    share = own.shape[0]
    for r, rows in enumerate((rows_mine, rows_theirs)):
        picked = []
        for s in range(slots):
            which, far = pos[r, s] // share, pos[r, s] % share
            block = jnp.zeros(own.shape[1:], BF16)
            block = jnp.where(which == 0, own[far], block)
            block = jnp.where(which == 1, beside[far], block)
            picked.append(block)
        out[r] = jnp.dot(rows[...], jnp.concatenate(picked, 0), preferred_element_type=F32)
    out[2] = cot[...].astype(F32)


def gradients(mine, theirs, weight, perm, activated, ordered, moved):
    tile = weight.shape[0]
    grad = jnp.zeros((tile, tile), F32)
    for r, cot in enumerate((mine, theirs)):
        mixed = mine[r] + theirs[1 - r]
        high = mixed.astype(BF16)
        low = (mixed - high.astype(F32)).astype(BF16)
        pre = jnp.dot(high, weight[...], preferred_element_type=F32) + jnp.dot(
            low, weight[...], preferred_element_type=F32
        )
        sig = jax.nn.sigmoid(pre)
        if r == 0:
            activated[...] = (pre * sig).astype(BF16)
        act_grad = (cot[2] * sig * (1.0 + pre * (1.0 - sig))).astype(BF16)
        moved[r] = lax.dot_general(
            act_grad, weight[...], (((1,), (1,)), ((), ())), preferred_element_type=F32
        ).astype(BF16)
        for part in (high, low):
            grad += lax.dot_general(
                part, act_grad, (((0,), (0,)), ((), ())), preferred_element_type=F32
            )
    top = grad.astype(BF16)
    rest = (grad - top.astype(F32)).astype(BF16)
    ordered[...] = jnp.dot(perm[...], top, preferred_element_type=F32) + jnp.dot(
        perm[...], rest, preferred_element_type=F32
    )


def backward(pos, moved, cols_mine, cols_theirs, out0, out1, out2, out3, total):
    slots = pos.shape[1]
    tile = moved.shape[1]
    blocks = total.shape[0] - 1
    total[...] = jnp.zeros_like(total)
    for r, cols in enumerate((cols_mine, cols_theirs)):
        for s in range(slots):
            total[pos[r, s]] += jnp.dot(
                cols[pl.ds(s * tile, tile), :], moved[r], preferred_element_type=F32
            )
    share = blocks // CLASSES
    for a, out in enumerate((out0, out1, out2, out3)):
        for k in range(share):
            out[k] = total[a * share + k].astype(BF16)


def shards(features, weight, tiles, tile_cols, tile_counts, cotangent):
    feat = features[0]
    tile = feat.shape[0]
    slots = tiles.shape[2]
    wide = lax.axis_size("wide")
    chips = wide // 2
    share = chips // CLASSES
    w = lax.axis_index("wide")
    z, c = w // 2, w % 2
    sign = 1 - 2 * c

    def send(x, d):
        return lax.ppermute(
            x, "wide",
            [(2 * i + k, 2 * ((i + (d if k == 0 else -d)) % chips) + k) for i in range(chips) for k in range(2)],
        )

    def swap(x):
        return lax.ppermute(x, "wide", [(i, i ^ 1) for i in range(wide)])

    def every(step):
        return [
            [2 * (m + k) + core for m in range(0, chips, step)] for k in range(step) for core in range(2)
        ]

    with jax.named_scope("gather_far"):
        held = lax.all_gather(feat, "wide", axis_index_groups=every(2))
    with jax.named_scope("gather_near"):
        beside = send(held, 1)
    with jax.named_scope("prepare"):
        after = lax.optimization_barrier(held[0, :8] + held[-1, :8])
        _, tiles, tile_cols, tile_counts = lax.optimization_barrier((after, tiles, tile_cols, tile_counts))
        other = swap(tiles)
        rows = [t[0].reshape(tile, slots * tile) for t in (tiles, other)]
        flipped = [r.T for r in rows]
        here = jnp.stack([w, w ^ 1])
        cols = tile_cols[0][here]
        counts = tile_counts[0][here]
        chip = cols // 2
        active = (jnp.arange(slots)[None, :] < counts[:, None]) & (cols % 2 == c)
        source = (z - chip) % 2 * (chips // 2) + chip // 2
        source = jnp.where(active, source, chips).astype(jnp.int32)
        place = (sign * (z - chip)) % CLASSES * share + chip // CLASSES
        place = jnp.where(active, place, chips).astype(jnp.int32)
        spot = jnp.arange(chips)
        chip_at = (z - sign * (spot // share)) % CLASSES + CLASSES * (spot % share)
        row_share = tile // wide
        row_at = ((2 * chip_at + c)[:, None] * row_share + jnp.arange(row_share)[None, :]).reshape(-1)
        perm = (row_at[:, None] == jnp.arange(tile)[None, :]).astype(BF16)
    mixed = pl.pallas_call(
        forward,
        out_shape=jax.ShapeDtypeStruct((3, tile, tile), F32),
        in_specs=[SMEM] + [VMEM] * 5,
        out_specs=VMEM,
        compiler_params=PARAMS,
        name="forward",
    )(source, held, beside, *rows, cotangent[0])
    with jax.named_scope("pair"):
        theirs = swap(mixed)
    activated, grad, moved = pl.pallas_call(
        gradients,
        out_shape=[
            jax.ShapeDtypeStruct((tile, tile), BF16),
            jax.ShapeDtypeStruct((tile // 2, tile), F32),
            jax.ShapeDtypeStruct((2, tile, tile), BF16),
        ],
        in_specs=[VMEM] * 4,
        out_specs=[VMEM] * 3,
        compiler_params=PARAMS,
        name="gradients",
    )(mixed, theirs, weight, perm)
    parts = pl.pallas_call(
        backward,
        out_shape=[jax.ShapeDtypeStruct((share, tile, tile), BF16)] * CLASSES,
        in_specs=[SMEM] + [VMEM] * 3,
        out_specs=[VMEM] * CLASSES,
        scratch_shapes=[pltpu.VMEM((chips + 1, tile, tile), F32)],
        compiler_params=PARAMS,
        name="backward",
    )(place, moved, *flipped)
    with jax.named_scope("weight_groups"):
        groups = lax.axis_size("narrow")
        grad = lax.all_to_all(jnp.broadcast_to(grad[None], (groups,) + grad.shape), "narrow", 0, 0).sum(0)
        grads = grad.reshape(CLASSES, share, row_share, tile)
    with jax.named_scope("scatter_near"):
        whole = parts[0].astype(F32)
        for part, d in zip(parts[1:], NEAR[1:]):
            whole += send(part, -d).astype(F32)
        main = whole.astype(BF16)
    with jax.named_scope("weight_near"):
        grad = grads[0]
        for a, d in list(enumerate(NEAR))[1:]:
            grad += send(grads[a], -d)
    with jax.named_scope("scatter_far"):
        top = grad.astype(BF16)
        rest = (grad - top.astype(F32)).astype(BF16)
        message = jnp.concatenate([main, top, rest], 1)
        got = lax.all_to_all(message, "wide", 0, 0, axis_index_groups=every(CLASSES))
        whole = got.astype(F32).sum(0)
        feature_grad = whole[:tile].astype(BF16)
        weight_grad = whole[tile : tile + row_share] + whole[tile + row_share :]
    return (activated[None], feature_grad[None], weight_grad)


def solution(mesh):
    placed = (
        P("narrow", "wide", None),
        P(),
        P("narrow", "wide", None, None),
        P("narrow", None, None),
        P("narrow", None),
        P("narrow", "wide", None),
    )
    return jax.shard_map(
        shards,
        mesh=mesh,
        in_specs=placed,
        out_specs=(P("narrow", "wide", None), P("narrow", "wide", None), P("wide", None)),
        check_vma=False,
    )
```
